256 devices in a mesh: dp: 16 (over x, y), mp: 16 (over z, core).
Axes of the slice: x: 4, y: 4, z: 8, core: 2. Of those that a mesh axis runs over, the one named last changes fastest.
Arguments:
- train_acts: bfloat16 [2048, 4096], P('dp', 'mp'), may hold values from -6 to 6
- train_grads: bfloat16 [2048, 7168], P('dp', 'mp'), may hold values from -0.75 to 0.75
- query_acts: bfloat16 [1024, 4096], P('dp', 'mp'), may hold values from -6 to 6
- query_grads: bfloat16 [1024, 7168], P('dp', 'mp'), may hold values from -0.75 to 0.75
- basis_in: bfloat16 [4096, 4096], P('mp'), may hold values from -0.125 to 0.125
- basis_out: bfloat16 [7168, 7168], P('mp'), may hold values from -0.09375 to 0.09375
- eigvals: bfloat16 [4096, 7168], P(None, 'mp'), may hold values from 0.25 to 4
Outputs:
- scores: float32 [16, 32], P(None, 'dp')
- energies: float32 [32], P('dp')
The draws below stay inside these ranges and needn't reach their ends.
All inputs are finite; a program needn't handle non-finite values.
Results may differ from the reference program's by a relative error of at most 0.0048.
Values may be sent and summed in bfloat16 or wider, within the bound.
A program may use at most 128 MiB of HBM per device.

```python
import math
import jax
import jax.numpy as jnp
from jax import lax

D = 4096
H = 7168
SEQ = 64
QSEQ = 16
TRAIN = 32
N_MP = 16


def strengthened(drawn, rng, source, target, parts, factor):
    def block_of(dim):
        return (jnp.arange(drawn.shape[dim]) // (drawn.shape[dim] // parts)).reshape((-1,) + (1,) * (drawn.ndim - 1 - dim))

    one_side = jax.random.permutation(rng, parts)[block_of(target)]
    second = (block_of(target) + parts // 2) % parts
    return jnp.where((block_of(source) == one_side) | (block_of(source) == second), factor * drawn, drawn)


def block_scale(rng, shape, cuts, smallest, high):
    loudness, own = 1.0, jax.random.fold_in(rng, 6)
    for axis_at, parts in cuts:
        heights = jnp.exp(jax.random.uniform(jax.random.fold_in(own, axis_at), (parts,), jnp.float32, smallest / len(cuts), high / len(cuts)))
        loudness = loudness * jnp.repeat(heights, shape[axis_at] // parts).reshape([-1 if axis == axis_at else 1 for axis in range(len(shape))])
    return loudness


def centred(key, extent, spread, bound, split=(), held_as=jnp.bfloat16):
    loudness = block_scale(key, extent, split, -0.22, 0.18) if split else 1.0
    values = jax.random.normal(key, extent, jnp.float32) * spread * loudness
    return jnp.minimum(jnp.maximum(values, -bound), bound).astype(held_as)


def heavy_noise(rng, dims, width, limit, split, heavy, kind=jnp.bfloat16):
    entries = width * jax.random.normal(rng, dims, jnp.float32)
    if split:
        entries = entries * block_scale(rng, dims, split, -0.22, 0.18)
    return jnp.clip(strengthened(entries, jax.random.fold_in(rng, 3), *heavy), -limit, limit).astype(kind)


def setup_inputs(seed: int = 0) -> dict:
    seeds = jax.random.split(jax.random.key(seed), 8)
    return {
        "train_acts": centred(seeds[0], (TRAIN * SEQ, D), 1.0, 6.0, ((0, 16), (1, 16))),
        "train_grads": centred(seeds[1], (TRAIN * SEQ, H), 0.125, 0.75, ((0, 16), (1, 16))),
        "query_acts": centred(seeds[2], (QSEQ * SEQ, D), 1.0, 6.0, ((0, 16), (1, 16))),
        "query_grads": centred(seeds[3], (QSEQ * SEQ, H), 0.125, 0.75, ((0, 16), (1, 16))),
        "basis_in": heavy_noise(seeds[4], (D, D), D ** -0.5, 0.125, ((0, 16),), (0, 1, 16, 2.0)),
        "basis_out": heavy_noise(seeds[5], (H, H), H ** -0.5, 0.09375, ((0, 16),), (0, 1, 16, 2.0)),
        "eigvals": jnp.clip(jnp.exp(math.log(4.0) - 2.7725887 * jax.random.uniform(seeds[6], (D, H), jnp.float32) ** block_scale(seeds[6], (D, H), ((1, 16),), -0.2, 0.2)), 0.25, 4.0).astype(jnp.bfloat16),
    }


damping = 0.1

def reference(train_acts, train_grads, query_acts, query_grads, basis_in, basis_out, eigvals):
    train_rot_a = jnp.dot(train_acts, basis_in, preferred_element_type=jnp.float32).astype(jnp.bfloat16).reshape(TRAIN, SEQ, D)
    query_rot_a = jnp.dot(query_acts, basis_in, preferred_element_type=jnp.float32).astype(jnp.bfloat16).reshape(QSEQ, SEQ, D)
    train_rot_g = jnp.dot(train_grads, basis_out, preferred_element_type=jnp.float32).astype(jnp.bfloat16).reshape(TRAIN, SEQ, H)
    query_rot_g = jnp.dot(query_grads, basis_out, preferred_element_type=jnp.float32).astype(jnp.bfloat16).reshape(QSEQ, SEQ, H)
    block_width = H // N_MP
    train_wide = train_rot_a.astype(jnp.float32)
    query_wide = query_rot_a.astype(jnp.float32)

    def one_block(block_index):
        offset = block_index * block_width
        train_part = lax.dynamic_slice_in_dim(train_rot_g, offset, block_width, 2).astype(jnp.float32)
        query_part = lax.dynamic_slice_in_dim(query_rot_g, offset, block_width, 2).astype(jnp.float32)
        shifted = lax.dynamic_slice_in_dim(eigvals, offset, block_width, 1).astype(jnp.float32) + damping
        train_outer = jnp.einsum('nsi,nsj->nij', train_wide, train_part)
        rounded = lax.optimization_barrier((train_outer / shifted).astype(jnp.bfloat16))
        scaled = rounded.astype(jnp.float32)
        query_outer = jnp.einsum('qsi,qsj->qij', query_wide, query_part)
        block_scores = jnp.einsum('qij,nij->qn', query_outer, scaled, precision=lax.Precision.HIGHEST)
        energy = lax.optimization_barrier(jnp.sum(train_outer * train_outer, axis=(1, 2)))
        return (block_scores, energy)
    pieces = lax.map(one_block, jnp.arange(N_MP, dtype=jnp.int32))
    scores = lax.optimization_barrier(jnp.sum(pieces[0], axis=0)) * (1.0 / math.sqrt(D * H))
    energies = lax.optimization_barrier(jnp.sum(pieces[1], axis=0)) / (D * H)
    return (scores, energies)
```

```python
import math

import jax
import jax.numpy as jnp
from jax import lax
from jax.experimental import pallas as pl
from jax.experimental.pallas import tpu as pltpu
from jax.sharding import PartitionSpec as P

D = 4096
H = 7168
SEQ = 64
DAMPING = 0.1
IB = 256
JB = 896
FG = 448
FA = 256
NQ = 32
NT = 64
NR = NQ + NT
HALF = NR // 2
BF = jnp.bfloat16
F32 = jnp.float32
MESH = pl.DeviceIdType.MESH


def dot(a, b):
    return jnp.dot(a, b, preferred_element_type=F32)


def kernel(
    ta_hbm, qa_hbm, tgt_hbm, qg_hbm, bi_hbm, bo_hbm, eig_hbm, out_ref,
    B, XG, TGT, TGS, PART, SIBS, SIBR, GPS, GSS, GPR, GSR, G96, QGS,
    ACT, BI, EIG, INV, APS, ASS, APR, ASR, RA, QAS, QAF, S, ACC, ENE, MSG, R1, R2, X2,
    load_sem, b_sem, swap_send, swap_recv, sib_send, sib_recv,
    gp_send, gp_recv, gs_send, gs_recv, ap_send, ap_recv, as_send, as_recv,
    xa_send, xa_recv, xg_send, xg_recv, qg_send, qg_recv, za_send, za_recv, qa_send, qa_recv,
    r1_send, r1_recv, r2_send, r2_recv,
):
    d = lax.axis_index("dp")
    m = lax.axis_index("mp")
    z = m // 2
    c = m % 2
    s = 1 - 2 * c
    o = 1 - c
    su = 4 - 3 * c
    sv = 1 + 3 * c
    u = (d // su) % 4
    v = (d // sv) % 4
    sib = (d, 2 * z + o)

    def zdev(delta):
        return (d, 2 * ((z + delta + 8) % 8) + c)

    def slot_at(du, dv):
        return ((u + du + 4) % 4) * su + ((v + dv + 4) % 4) * sv

    def dpdev(du, dv):
        return (slot_at(du, dv), m)

    def remote(src, dst, send, recv, dev):
        return pltpu.make_async_remote_copy(
            src_ref=src, dst_ref=dst, send_sem=send, recv_sem=recv, device_id=dev, device_id_type=MESH
        )

    sends = []

    def push(src, dst, send, recv, dev):
        copy = remote(src, dst, send, recv, dev)
        copy.start()
        sends.append(copy)

    def arrived(dst, recv):
        remote(dst, dst, recv, recv, sib).wait_recv()

    def zoff(k):
        h = (k + 1) // 2
        return (4 - h) * (2 * (k % 2) - 1)

    def target(k):
        return (z + zoff(k) + 8) % 8

    loads = []

    def load(src, dst, sem):
        copy = pltpu.make_async_copy(src, dst, sem)
        copy.start()
        loads.append(copy)
        return copy

    own_cols = pl.ds(pl.multiple_of(c * FA, FA), FA)
    i_cols = pl.ds(pl.multiple_of(d * IB, IB), IB)

    def rows(cls, size):
        return pl.ds(pl.multiple_of(cls * size, size), size)

    l_tgt = load(tgt_hbm, TGT, load_sem.at[0])
    l_qg0 = load(qg_hbm.at[rows(c, NQ)], XG.at[pl.ds(0, NQ)], load_sem.at[1])
    l_qg1 = load(qg_hbm.at[rows(o, NQ)], XG.at[pl.ds(NR, NQ)], load_sem.at[2])
    b_loads = []
    for k in range(8):
        col = pl.multiple_of(target(k) * JB, 128)
        b_loads.append(load(bo_hbm.at[:, pl.ds(col, JB)], B.at[k], b_sem.at[k]))
    l_ta = load(ta_hbm.at[rows(c, NT)], ACT.at[d, pl.ds(NQ, NT), own_cols], load_sem.at[3])
    l_qa = load(qa_hbm.at[rows(c, NQ)], ACT.at[d, pl.ds(0, NQ), own_cols], load_sem.at[4])
    l_bi = load(bi_hbm.at[:, i_cols], BI.at[own_cols], load_sem.at[5])
    eig_rows = pl.ds(pl.multiple_of(c * FG, FG), FG)
    l_eig = load(eig_hbm.at[:, i_cols], EIG.at[eig_rows], load_sem.at[6])

    barrier = pltpu.get_barrier_semaphore()
    for k in range(1, 16):
        pl.semaphore_signal(barrier, inc=1, device_id=((d + k) % 16, m), device_id_type=MESH)
        pl.semaphore_signal(barrier, inc=1, device_id=(d, (m + k) % 16), device_id_type=MESH)
    pl.semaphore_wait(barrier, 30)

    push(ta_hbm.at[rows(o, NT)], ACT.at[d, pl.ds(NQ, NT), own_cols], swap_send.at[0], swap_recv.at[0], sib)
    push(qa_hbm.at[rows(o, NQ)], ACT.at[d, pl.ds(0, NQ), own_cols], swap_send.at[1], swap_recv.at[1], sib)
    push(bi_hbm.at[:, i_cols], BI.at[own_cols], swap_send.at[2], swap_recv.at[2], sib)
    push(eig_hbm.at[:, i_cols], EIG.at[eig_rows], swap_send.at[3], swap_recv.at[3], sib)
    sib_cols = pl.ds(pl.multiple_of(o * FA, FA), FA)

    l_tgt.wait()
    TGS[...] = jnp.transpose(TGT[...].astype(F32)).astype(BF)
    XG[pl.ds(NQ, NT), :] = TGS[rows(c, NT), :]
    XG[pl.ds(NR + NQ, NT), :] = TGS[rows(o, NT), :]
    l_qg0.wait()
    l_qg1.wait()

    def g_partial(k):
        b_loads[k].wait()
        part = dot(XG[...], B[k])
        PART[k] = part[:NR]
        SIBS[k] = part[NR:]
        push(SIBS.at[k], SIBR.at[k], sib_send.at[k], sib_recv.at[k], sib)

    def gather_stages(buf, send, recv):
        count = [0]

        def go(slot, dev):
            push(buf.at[slot], buf.at[slot], send.at[count[0]], recv.at[slot], dev)
            count[0] += 1

        def got(slot):
            arrived(buf.at[slot], recv.at[slot])

        def along_v(du):
            go(slot_at(du, 0), dpdev(0, 1))
            go(slot_at(du, 0), dpdev(0, -1))

        def stage_a():
            go(slot_at(0, 0), dpdev(s, 0))
            go(slot_at(0, 0), dpdev(-s, 0))
            along_v(0)
            return []

        def stage_b():
            got(slot_at(-s, 0))
            go(slot_at(-s, 0), dpdev(s, 0))
            along_v(-s)
            got(slot_at(s, 0))
            along_v(s)
            return [slot_at(-s, 0), slot_at(s, 0)]

        def stage_c():
            got(slot_at(0, -1))
            go(slot_at(0, -1), dpdev(0, 1))
            got(slot_at(0, 1))
            got(slot_at(2, 0))
            along_v(2)
            return [slot_at(0, -1), slot_at(0, 1), slot_at(2, 0)]

        def stage_d():
            done = []
            for du in (-s, s):
                got(slot_at(du, 1))
                go(slot_at(du, 1), dpdev(0, -1))
                got(slot_at(du, -1))
                done += [slot_at(du, 1), slot_at(du, -1)]
            return done

        def stage_e():
            got(slot_at(2, -1))
            go(slot_at(2, -1), dpdev(0, 1))
            got(slot_at(2, 1))
            got(slot_at(0, 2))
            return [slot_at(2, -1), slot_at(2, 1), slot_at(0, 2)]

        def stage_f():
            done = []
            for du in (-s, s, 2):
                got(slot_at(du, 2))
                done.append(slot_at(du, 2))
            return done

        return [stage_a, stage_b, stage_c, stage_d, stage_e, stage_f]

    xa = gather_stages(ACT, xa_send, xa_recv)
    xg = gather_stages(G96, xg_send, xg_recv)

    def g_query_to_sibling(slots):
        for slot in slots:
            push(G96.at[slot, pl.ds(0, NQ)], QGS.at[slot], qg_send.at[slot], qg_recv.at[slot], sib)

    def g_own(k, h):
        part = pl.ds(h * HALF, HALF)
        return PART[k, part, :] + SIBR[k, part, :]

    def g_ring(step):
        kp = 0 if step == 0 else 2 * step - 1 + c
        arrived(SIBR.at[kp], sib_recv.at[kp])
        if step < 3:
            ks = 2 * (step + 1) - c
            arrived(SIBR.at[ks], sib_recv.at[ks])
        for h in range(2):
            part = pl.ds(h * HALF, HALF)
            total = g_own(kp, h)
            if step > 0:
                arrived(GPR.at[step - 1, part], gp_recv.at[step - 1, h])
                total = total + GPR[step - 1, part, :].astype(F32)
            GPS[step, part, :] = total.astype(BF)
            push(GPS.at[step, part], GPR.at[step, part], gp_send.at[step, h], gp_recv.at[step, h], zdev(s))
            if step < 3:
                total = g_own(ks, h)
                if step > 0:
                    arrived(GSR.at[step - 1, part], gs_recv.at[step - 1, h])
                    total = total + GSR[step - 1, part, :].astype(F32)
                GSS[step, part, :] = total.astype(BF)
                push(GSS.at[step, part], GSR.at[step, part], gs_send.at[step, h], gs_recv.at[step, h], zdev(-s))

    def g_final():
        arrived(SIBR.at[7], sib_recv.at[7])
        for h in range(2):
            part = pl.ds(h * HALF, HALF)
            total = g_own(7, h)
            arrived(GSR.at[2, part], gs_recv.at[2, h])
            total = total + GSR[2, part, :].astype(F32)
            arrived(GPR.at[3, part], gp_recv.at[3, h])
            total = total + GPR[3, part, :].astype(F32)
            G96[d, part, :] = total.astype(BF)

    def a_own(delta, h):
        slot = 2 * ((z + delta + 8) % 8) + h
        return dot(ACT[slot], BI[...])

    def a_ring(step):
        for h in range(2):
            total = a_own(s * (4 - step), h)
            if step > 0:
                arrived(APR.at[step - 1, h], ap_recv.at[step - 1, h])
                total = total + APR[step - 1, h]
            APS[step, h] = total
            push(APS.at[step, h], APR.at[step, h], ap_send.at[step, h], ap_recv.at[step, h], zdev(s))
            if step < 3:
                total = a_own(-s * (3 - step), h)
                if step > 0:
                    arrived(ASR.at[step - 1, h], as_recv.at[step - 1, h])
                    total = total + ASR[step - 1, h]
                ASS[step, h] = total
                push(ASS.at[step, h], ASR.at[step, h], as_send.at[step, h], as_recv.at[step, h], zdev(-s))

    def a_final():
        for h in range(2):
            total = a_own(0, h)
            arrived(ASR.at[2, h], as_recv.at[2, h])
            total = total + ASR[2, h]
            arrived(APR.at[3, h], ap_recv.at[3, h])
            total = total + APR[3, h]
            RA[2 * z + h] = total.astype(BF)

    kind_rows = (pl.ds(0, NQ), pl.ds(NQ, NT))

    def za_ref(delta, kind):
        block = (z + delta + 8) % 8
        return RA.at[pl.ds(2 * block, 2), kind_rows[kind]]

    def za_index(delta):
        return (z + delta + 8) % 8

    za_count = [0]

    def za_go(delta, kind, dev):
        ref = za_ref(delta, kind)
        push(ref, ref, za_send.at[za_count[0]], za_recv.at[za_index(delta), kind], dev)
        za_count[0] += 1

    def za_got(delta, kind):
        arrived(za_ref(delta, kind), za_recv.at[za_index(delta), kind])

    def za_share(delta):
        block = za_index(delta)
        push(za_ref(delta, 0), QAS.at[pl.ds(2 * block, 2)], qa_send.at[block], qa_recv.at[block], sib)

    g_partial(0)
    g_partial(1)
    g_partial(2)
    g_ring(0)
    l_ta.wait()
    l_qa.wait()
    arrived(ACT.at[d, pl.ds(NQ, NT), sib_cols], swap_recv.at[0])
    arrived(ACT.at[d, pl.ds(0, NQ), sib_cols], swap_recv.at[1])
    xa[0]()
    g_partial(3)
    g_partial(4)
    xa[1]()
    g_ring(1)
    g_partial(5)
    g_partial(6)
    g_partial(7)
    xa[2]()
    g_ring(2)
    xa[3]()
    l_bi.wait()
    l_eig.wait()
    sib_eig = pl.ds(pl.multiple_of(o * FG, FG), FG)
    arrived(BI.at[sib_cols], swap_recv.at[2])
    arrived(EIG.at[sib_eig], swap_recv.at[3])
    INV[...] = 1.0 / (EIG[...].astype(F32) + DAMPING)
    xa[4]()
    g_ring(3)
    xa[5]()
    a_ring(0)
    g_final()
    xg[0]()
    g_query_to_sibling([d])
    a_ring(1)
    g_query_to_sibling(xg[1]())
    a_ring(2)
    g_query_to_sibling(xg[2]())
    a_ring(3)
    g_query_to_sibling(xg[3]())
    a_final()
    za_go(0, 0, zdev(s))
    za_go(0, 0, zdev(-s))
    za_go(0, 1, zdev(s))
    za_go(0, 1, zdev(-s))
    za_share(0)
    g_query_to_sibling(xg[4]())
    for step in (1, 2, 3):
        for kind in range(2):
            za_got(-s * step, kind)
            za_go(-s * step, kind, zdev(s))
            za_got(s * step, kind)
            if step < 3:
                za_go(s * step, kind, zdev(-s))
            if kind == 0:
                za_share(-s * step)
                za_share(s * step)
    g_query_to_sibling(xg[5]())
    for kind in range(2):
        za_got(4, kind)
    za_share(4)
    for k in range(16):
        arrived(QGS.at[k], qg_recv.at[k])
    for k in range(8):
        arrived(QAS.at[pl.ds(2 * k, 2)], qa_recv.at[k])

    QAF[0] = RA[:, pl.ds(0, NQ), :].reshape(16 * NQ, IB).astype(F32)
    QAF[1] = QAS[...].reshape(16 * NQ, IB).astype(F32)

    def one_train(slot, carry):
        acts = RA[slot, pl.ds(NQ, NT), :]
        energy = jnp.zeros((8, 128), F32)
        for j in range(JB // 128):
            cols = pl.ds(j * 128, 128)
            outer = lax.dot_general(
                G96[slot, pl.ds(NQ, NT), cols], acts, (((0,), (0,)), ((), ())), preferred_element_type=F32
            )
            square = outer * outer
            energy = energy + jnp.sum((square[:, :128] + square[:, 128:]).reshape(16, 8, 128), axis=0)
            S[cols, :] = (outer * INV[cols, :]).astype(BF)
        ENE[slot] = energy
        total = jnp.zeros((16, 8, 128), F32)
        for cls in range(2):
            grads = G96[:, pl.ds(0, NQ), :] if cls == 0 else QGS[...]
            applied = dot(grads.reshape(16 * NQ, JB), S[...]) * QAF[cls]
            total = total + jnp.sum((applied[:, :128] + applied[:, 128:]).reshape(16, NQ // 8, 8, 128), axis=1)
        ACC[slot] = total.reshape(128, 128)
        return carry

    lax.fori_loop(0, 16, one_train, 0)

    ones = jnp.ones((8, 128), F32)
    for n in range(16):
        MSG[n, pl.ds(0, 8), :] = lax.dot_general(
            ones, ACC[n], (((1,), (1,)), ((), ())), precision=lax.Precision.HIGHEST, preferred_element_type=F32
        )
        MSG[n, pl.ds(8, 8), :] = ENE[n]
    R1[d] = MSG[d]
    for k in range(1, 16):
        peer = (d + k) % 16
        push(MSG.at[peer], R1.at[d], r1_send.at[k], r1_recv.at[d], (peer, m))
    for k in range(1, 16):
        peer = (d + k) % 16
        arrived(R1.at[peer], r1_recv.at[peer])
    X2[...] = jnp.sum(R1[...], axis=0)
    R2[m] = X2[...]
    for k in range(1, 16):
        peer = (m + k) % 16
        push(X2, R2.at[m], r2_send.at[k], r2_recv.at[m], (d, peer))
    for k in range(1, 16):
        peer = (m + k) % 16
        arrived(R2.at[peer], r2_recv.at[peer])
    for cls in range(2):
        total = R2[cls]
        for k in range(1, 8):
            total = total + R2[2 * k + cls]
        out_ref[cls] = total
    for copy in sends:
        copy.wait_send()


def on_device(train_acts, train_grads, query_acts, query_grads, basis_in, basis_out, eigvals):
    dma = pltpu.SemaphoreType.DMA
    vm = pltpu.VMEM
    sums = pl.pallas_call(
        kernel,
        out_shape=jax.ShapeDtypeStruct((2, 16, 128), F32),
        in_specs=[pl.BlockSpec(memory_space=pl.ANY)] * 7,
        out_specs=pl.BlockSpec(memory_space=pltpu.VMEM),
        scratch_shapes=[
            vm((8, FG, JB), BF),
            vm((2 * NR, FG), BF),
            vm((FG, 128), BF),
            vm((128, FG), BF),
            vm((8, NR, JB), F32),
            vm((8, NR, JB), F32),
            vm((8, NR, JB), F32),
            vm((4, NR, JB), BF),
            vm((3, NR, JB), BF),
            vm((4, NR, JB), BF),
            vm((3, NR, JB), BF),
            vm((16, NR, JB), BF),
            vm((16, NQ, JB), BF),
            vm((16, NR, 2 * FA), BF),
            vm((2 * FA, IB), BF),
            vm((JB, IB), BF),
            vm((JB, IB), F32),
            vm((4, 2, NR, IB), F32),
            vm((3, 2, NR, IB), F32),
            vm((4, 2, NR, IB), F32),
            vm((3, 2, NR, IB), F32),
            vm((16, NR, IB), BF),
            vm((16, NQ, IB), BF),
            vm((2, 16 * NQ, IB), F32),
            vm((JB, IB), BF),
            vm((16, 128, 128), F32),
            vm((16, 8, 128), F32),
            vm((16, 16, 128), F32),
            vm((16, 16, 128), F32),
            vm((16, 16, 128), F32),
            vm((16, 128), F32),
            dma((7,)), dma((8,)), dma((4,)), dma((4,)), dma((8,)), dma((8,)),
            dma((4, 2)), dma((4, 2)), dma((3, 2)), dma((3, 2)),
            dma((4, 2)), dma((4, 2)), dma((3, 2)), dma((3, 2)),
            dma((15,)), dma((16,)), dma((15,)), dma((16,)), dma((16,)), dma((16,)),
            dma((14,)), dma((8, 2)), dma((8,)), dma((8,)),
            dma((16,)), dma((16,)), dma((16,)), dma((16,)),
        ],
        compiler_params=pltpu.CompilerParams(
            collective_id=0, has_side_effects=True, vmem_limit_bytes=56 * 1024 * 1024
        ),
        cost_estimate=pl.CostEstimate(flops=10_000_000_000, bytes_accessed=8_000_000, transcendentals=0),
    )(train_acts, query_acts, train_grads.T, query_grads, basis_in, basis_out, eigvals.T)
    scores = jnp.sum(sums[:, 0, :].reshape(2, 16, 8), axis=2).T * (1.0 / math.sqrt(D * H))
    energies = jnp.sum(sums[:, 8:, :], axis=(1, 2)) / (D * H)
    return (scores, energies)


def solution(mesh):
    return jax.shard_map(
        on_device,
        mesh=mesh,
        in_specs=(
            P("dp", "mp"),
            P("dp", "mp"),
            P("dp", "mp"),
            P("dp", "mp"),
            P("mp", None),
            P("mp", None),
            P(None, "mp"),
        ),
        out_specs=(P(None, "dp"), P("dp")),
        check_vma=False,
    )
```

```python
import math

import jax
import jax.numpy as jnp
from jax import lax
from jax.experimental import pallas as pl
from jax.experimental.pallas import tpu as pltpu
from jax.sharding import PartitionSpec as P

D = 4096
H = 7168
SEQ = 64
DAMPING = 0.1
IB = 256
JB = 896
FG = 448
FA = 256
NQ = 32
NT = 64
NR = NQ + NT
CUTS = 3
KINDS = NR // NQ
CUT = NR // CUTS
BF = jnp.bfloat16
F32 = jnp.float32
MESH = pl.DeviceIdType.MESH


def dot(a, b):
    return jnp.dot(a, b, preferred_element_type=F32)


def kernel(
    ta_hbm, qa_hbm, tgt_hbm, qg_hbm, bi_hbm, bo_hbm, eig_hbm, sc_ref, en_ref,
    B, XG, TGT, TGS, PART, SIBS, SIBR, GPS, GSS, GPR, GSR, G96, QGS,
    ACT, BI, EIG, INV, APART, APS, ASS, APR, ASR, RA, QAS, S, MSG, R1, R2, X2, R3,
    load_sem, b_sem, swap_send, swap_recv, sib_send, sib_recv,
    gp_send, gp_recv, gs_send, gs_recv, ap_send, ap_recv, as_send, as_recv,
    xa_send, xa_recv, xg_send, xg_recv, qg_send, qg_recv, za_send, za_recv, qa_send, qa_recv,
    r1_send, r1_recv, r2_send, r2_recv, r3_send, r3_recv,
):
    d = lax.axis_index("dp")
    m = lax.axis_index("mp")
    z = m // 2
    c = m % 2
    s = 1 - 2 * c
    o = 1 - c
    su = 4 - 3 * c
    sv = 1 + 3 * c
    u = (d // su) % 4
    v = (d // sv) % 4
    sib = (d, 2 * z + o)

    def zat(delta):
        return (z + delta + 8) % 8

    def zdev(delta):
        return (d, 2 * zat(delta) + c)

    def slot_at(du, dv):
        return ((u + du + 4) % 4) * su + ((v + dv + 4) % 4) * sv

    def dpdev(du, dv):
        return (slot_at(du, dv), m)

    def remote(src, dst, send, recv, dev):
        return pltpu.make_async_remote_copy(
            src_ref=src, dst_ref=dst, send_sem=send, recv_sem=recv, device_id=dev, device_id_type=MESH
        )

    sends = []

    def push(src, dst, send, recv, dev):
        copy = remote(src, dst, send, recv, dev)
        copy.start()
        sends.append(copy)

    def arrived(dst, recv):
        remote(dst, dst, recv, recv, sib).wait_recv()

    barrier = pltpu.get_barrier_semaphore()
    greeted = [sib, zdev(1), zdev(-1)] + [dpdev(k, 0) for k in (1, 2, 3)] + [dpdev(0, k) for k in (1, 2, 3)]
    for dev in greeted:
        pl.semaphore_signal(barrier, inc=1, device_id=dev, device_id_type=MESH)

    def zoff(k):
        h = (k + 1) // 2
        return (4 - h) * (2 * (k % 2) - 1)

    def target(k):
        return (z + zoff(k) + 8) % 8

    loads = []

    def load(src, dst, sem):
        copy = pltpu.make_async_copy(src, dst, sem)
        copy.start()
        loads.append(copy)
        return copy

    own_cols = pl.ds(pl.multiple_of(c * FA, FA), FA)
    i_cols = pl.ds(pl.multiple_of(d * IB, IB), IB)

    def rows(cls, size):
        return pl.ds(pl.multiple_of(cls * size, size), size)

    l_tgt = load(tgt_hbm, TGT, load_sem.at[0])
    l_qg0 = load(qg_hbm.at[rows(c, NQ)], XG.at[pl.ds(0, NQ)], load_sem.at[1])
    l_qg1 = load(qg_hbm.at[rows(o, NQ)], XG.at[pl.ds(NR, NQ)], load_sem.at[2])
    b_loads = []
    for k in range(8):
        col = pl.multiple_of(target(k) * JB, 128)
        b_loads.append(load(bo_hbm.at[:, pl.ds(col, JB)], B.at[k], b_sem.at[k]))
    l_ta = load(ta_hbm.at[rows(c, NT)], ACT.at[d, pl.ds(NQ, NT), own_cols], load_sem.at[3])
    l_qa = load(qa_hbm.at[rows(c, NQ)], ACT.at[d, pl.ds(0, NQ), own_cols], load_sem.at[4])
    l_bi = load(bi_hbm.at[:, i_cols], BI.at[own_cols], load_sem.at[5])
    eig_rows = pl.ds(pl.multiple_of(c * FG, FG), FG)
    l_eig = load(eig_hbm.at[:, i_cols], EIG.at[eig_rows], load_sem.at[6])

    sib_cols = pl.ds(pl.multiple_of(o * FA, FA), FA)

    l_tgt.wait()
    TGS[...] = jnp.transpose(TGT[...].astype(F32)).astype(BF)
    XG[pl.ds(NQ, NT), :] = TGS[rows(c, NT), :]
    XG[pl.ds(NR + NQ, NT), :] = TGS[rows(o, NT), :]
    l_qg0.wait()
    l_qg1.wait()

    def swap_inputs():
        push(ta_hbm.at[rows(o, NT)], ACT.at[d, pl.ds(NQ, NT), own_cols], swap_send.at[0], swap_recv.at[0], sib)
        push(qa_hbm.at[rows(o, NQ)], ACT.at[d, pl.ds(0, NQ), own_cols], swap_send.at[1], swap_recv.at[1], sib)
        push(bi_hbm.at[:, i_cols], BI.at[own_cols], swap_send.at[2], swap_recv.at[2], sib)
        push(eig_hbm.at[:, i_cols], EIG.at[eig_rows], swap_send.at[3], swap_recv.at[3], sib)

    def g_partial(k):
        b_loads[k].wait()
        part = dot(XG[...], B[k])
        PART[k] = part[:NR]
        SIBS[k] = part[NR:]

    def g_swap(k):
        push(SIBS.at[k], SIBR.at[k], sib_send.at[k], sib_recv.at[k], sib)

    def make_gather(buf, send, recv, landed):
        count = [0]

        def go(slot, dev):
            push(buf.at[slot], buf.at[slot], send.at[count[0]], recv.at[slot], dev)
            count[0] += 1

        def along_v(du):
            for dv in (1, 3, 2):
                go(slot_at(du, 0), dpdev(0, dv))

        def start():
            for du in (1, 3, 2):
                go(slot_at(0, 0), dpdev(du, 0))
            along_v(0)
            landed(slot_at(0, 0))

        def got(du, dv):
            slot = slot_at(du, dv)
            arrived(buf.at[slot], recv.at[slot])
            if dv == 0:
                along_v(du)
            landed(slot)

        return start, got

    def g_query_to_sibling(slot):
        push(G96.at[slot, pl.ds(0, NQ)], QGS.at[slot], qg_send.at[slot], qg_recv.at[slot], sib)

    xa_start, xa_got = make_gather(ACT, xa_send, xa_recv, lambda slot: None)
    xg_start, xg_got = make_gather(G96, xg_send, xg_recv, g_query_to_sibling)

    def g_own(k, h):
        part = pl.ds(h * CUT, CUT)
        return PART[k, part, :] + SIBR[k, part, :]

    def g_ring(step):
        kp = 0 if step == 0 else 2 * step - 1 + c
        arrived(SIBR.at[kp], sib_recv.at[kp])
        if step < 3:
            ks = 2 * (step + 1) - c
            arrived(SIBR.at[ks], sib_recv.at[ks])
        for h in range(CUTS):
            part = pl.ds(h * CUT, CUT)
            total = g_own(kp, h)
            if step > 0:
                arrived(GPR.at[step - 1, part], gp_recv.at[step - 1, h])
                total = total + GPR[step - 1, part, :].astype(F32)
            GPS[step, part, :] = total.astype(BF)
            push(GPS.at[step, part], GPR.at[step, part], gp_send.at[step, h], gp_recv.at[step, h], zdev(s))
            if step < 3:
                total = g_own(ks, h)
                if step > 0:
                    arrived(GSR.at[step - 1, part], gs_recv.at[step - 1, h])
                    total = total + GSR[step - 1, part, :].astype(F32)
                GSS[step, part, :] = total.astype(BF)
                push(GSS.at[step, part], GSR.at[step, part], gs_send.at[step, h], gs_recv.at[step, h], zdev(-s))

    def g_final():
        arrived(SIBR.at[7], sib_recv.at[7])
        for h in range(CUTS):
            part = pl.ds(h * CUT, CUT)
            total = g_own(7, h)
            arrived(GSR.at[2, part], gs_recv.at[2, h])
            total = total + GSR[2, part, :].astype(F32)
            arrived(GPR.at[3, part], gp_recv.at[3, h])
            total = total + GPR[3, part, :].astype(F32)
            G96[d, part, :] = total.astype(BF)

    kind_rows = tuple(pl.ds(k * NQ, NQ) for k in range(KINDS))

    def a_local(delta):
        block = zat(delta)
        both = dot(ACT[pl.ds(2 * block, 2)].reshape(2 * NR, 2 * FA), BI[...])
        APART[block] = both.reshape(2, NR, IB)

    def a_own(delta, kind):
        return APART[zat(delta), :, kind_rows[kind], :].reshape(2 * NQ, IB)

    def a_step(i):
        if i == 0:
            a_local(4 * s)
            a_local(-3 * s)
        for kind in range(KINDS):
            total = a_own(s * (4 - i), kind)
            if i > 0:
                arrived(APR.at[kind, i - 1], ap_recv.at[kind, i - 1])
                total = total + APR[kind, i - 1]
            APS[kind, i] = total
            push(APS.at[kind, i], APR.at[kind, i], ap_send.at[kind, i], ap_recv.at[kind, i], zdev(s))
            if i < 3:
                total = a_own(-s * (3 - i), kind)
                if i > 0:
                    arrived(ASR.at[kind, i - 1], as_recv.at[kind, i - 1])
                    total = total + ASR[kind, i - 1]
                ASS[kind, i] = total
                push(ASS.at[kind, i], ASR.at[kind, i], as_send.at[kind, i], as_recv.at[kind, i], zdev(-s))
        if i == 0:
            for delta in (3 * s, -2 * s, 2 * s, -s, s, 0):
                a_local(delta)

    def a_final(kind):
        total = a_own(0, kind)
        arrived(ASR.at[kind, 2], as_recv.at[kind, 2])
        total = total + ASR[kind, 2]
        arrived(APR.at[kind, 3], ap_recv.at[kind, 3])
        total = total + APR[kind, 3]
        RA[pl.ds(2 * z, 2), kind_rows[kind], :] = total.astype(BF).reshape(2, NQ, IB)

    def za_ref(delta, kind):
        block = (z + delta + 8) % 8
        return RA.at[pl.ds(2 * block, 2), kind_rows[kind]]

    def za_index(delta):
        return (z + delta + 8) % 8

    za_count = [0]

    def za_go(delta, kind, dev):
        ref = za_ref(delta, kind)
        push(ref, ref, za_send.at[za_count[0]], za_recv.at[za_index(delta), kind], dev)
        za_count[0] += 1

    def za_got(delta, kind):
        arrived(za_ref(delta, kind), za_recv.at[za_index(delta), kind])

    def za_share(delta):
        block = za_index(delta)
        push(za_ref(delta, 0), QAS.at[pl.ds(2 * block, 2)], qa_send.at[block], qa_recv.at[block], sib)

    def za_start(kind):
        za_go(0, kind, zdev(s))
        za_go(0, kind, zdev(-s))
        if kind == 0:
            za_share(0)

    def za_step(kind, step):
        za_got(-s * step, kind)
        if step < 4:
            za_go(-s * step, kind, zdev(s))
            za_got(s * step, kind)
            if step < 3:
                za_go(s * step, kind, zdev(-s))
        if kind == 0:
            za_share(-s * step)
            if step < 4:
                za_share(s * step)

    def outers(delta):
        def one(h, carry):
            slot = 2 * za_index(delta) + h
            acts = RA[slot, pl.ds(NQ, NT), :]
            energy = jnp.zeros((8, 128), F32)
            for j in range(JB // 128):
                cols = pl.ds(j * 128, 128)
                outer = lax.dot_general(
                    G96[slot, pl.ds(NQ, NT), cols], acts, (((0,), (0,)), ((), ())), preferred_element_type=F32
                )
                square = outer * outer
                energy = energy + jnp.sum((square[:, :128] + square[:, 128:]).reshape(16, 8, 128), axis=0)
                S[slot, cols, :] = (outer * INV[cols, :]).astype(BF)
            MSG[slot, pl.ds(16, 8), :] = energy
            return carry

        lax.fori_loop(0, 2, one, 0)

    def scores_of(slot):
        total = jnp.zeros((16, 8, 128), F32)
        for cls in range(2):
            grads = G96[:, pl.ds(0, NQ), :] if cls == 0 else QGS[...]
            acts = RA[:, pl.ds(0, NQ), :] if cls == 0 else QAS[...]
            applied = dot(grads.reshape(16 * NQ, JB), S[slot]) * acts.reshape(16 * NQ, IB).astype(F32)
            total = total + jnp.sum((applied[:, :128] + applied[:, 128:]).reshape(16, NQ // 8, 8, 128), axis=1)
        MSG[slot, pl.ds(0, 16), :] = jnp.sum(total, axis=1)

    def z_step(i):
        for kind in range(KINDS):
            za_step(kind, i)

    for k in (0, 1, 2):
        g_partial(k)
    pl.semaphore_wait(barrier, len(greeted))
    swap_inputs()
    for k in (0, 1, 2):
        g_swap(k)
    g_ring(0)
    l_ta.wait()
    l_qa.wait()
    arrived(ACT.at[d, pl.ds(NQ, NT), sib_cols], swap_recv.at[0])
    arrived(ACT.at[d, pl.ds(0, NQ), sib_cols], swap_recv.at[1])
    xa_start()
    for k in range(3, 8):
        g_partial(k)
        g_swap(k)
    g_ring(1)
    xa_got(1, 0)
    xa_got(3, 0)
    l_bi.wait()
    l_eig.wait()
    sib_eig = pl.ds(pl.multiple_of(o * FG, FG), FG)
    arrived(BI.at[sib_cols], swap_recv.at[2])
    arrived(EIG.at[sib_eig], swap_recv.at[3])
    INV[...] = 1.0 / (EIG[...].astype(F32) + DAMPING)
    xa_got(2, 0)
    g_ring(2)
    for du in (0, 1, 3, 2):
        if du == 2:
            g_ring(3)
        for dv in (1, 3, 2):
            xa_got(du, dv)
    a_step(0)
    g_final()
    xg_start()
    a_step(1)
    xg_got(1, 0)
    xg_got(3, 0)
    xg_got(2, 0)
    a_step(2)
    for dv in (1, 3, 2):
        xg_got(0, dv)
    a_step(3)
    for du in (1, 3):
        for dv in (1, 3, 2):
            xg_got(du, dv)
    for kind in range(KINDS):
        a_final(kind)
        za_start(kind)
    for dv in (1, 3, 2):
        xg_got(2, dv)
    outers(0)
    z_step(1)
    outers(1)
    outers(-1)
    z_step(2)
    outers(2)
    outers(-2)
    z_step(3)
    outers(3)
    outers(-3)
    z_step(4)
    outers(4)
    for k in range(16):
        arrived(QGS.at[k], qg_recv.at[k])
    for k in range(8):
        arrived(QAS.at[pl.ds(2 * k, 2)], qa_recv.at[k])

    def far(a):
        return (2 - a + 3 * (a // 2) + 2 * (a // 3) + 8) % 4

    def r1_copy(p):
        peer = slot_at(far(p // 4), far(p % 4))
        return remote(MSG.at[peer], R1.at[d], r1_send.at[p], r1_recv.at[d], (peer, m)), peer

    def one_train(p, carry):
        copy, peer = r1_copy(p)
        scores_of(peer)
        copy.start()
        return carry

    lax.fori_loop(0, 15, one_train, 0)
    scores_of(d)
    R1[d] = MSG[d]
    for k in range(1, 16):
        peer = (d + k) % 16
        arrived(R1.at[peer], r1_recv.at[peer])

    def over_lanes(x):
        return lax.dot_general(
            jnp.ones((8, 128), F32), x, (((1,), (1,)), ((), ())), precision=lax.Precision.HIGHEST,
            preferred_element_type=F32,
        )

    X2[...] = jnp.zeros((8, 128), F32)
    X2[:, pl.ds(0, 24)] = over_lanes(jnp.sum(R1[...], axis=0))
    R2[z] = X2[...]
    for delta in (4, 3, -3, 2, -2, 1, -1):
        push(X2, R2.at[z], r2_send.at[delta + 3], r2_recv.at[z], zdev(delta))
    for delta in (1, -1, 2, -2, 3, -3, 4):
        arrived(R2.at[zat(delta)], r2_recv.at[zat(delta)])
    R3[c] = jnp.sum(R2[...], axis=0)
    push(R3.at[c], R3.at[c], r3_send, r3_recv, sib)
    arrived(R3.at[o], r3_recv)
    for cls in range(2):
        sc_ref[pl.ds(cls, 1), :] = R3[cls, :1, :16]
        en_ref[:, pl.ds(cls, 1)] = jnp.sum(R3[cls, :1, 16:24], axis=1, keepdims=True)
    for copy in sends:
        copy.wait_send()
    for p in range(15):
        r1_copy(p)[0].wait_send()


def on_device(train_acts, train_grads, query_acts, query_grads, basis_in, basis_out, eigvals):
    dma = pltpu.SemaphoreType.DMA
    vm = pltpu.VMEM
    scores, energies = pl.pallas_call(
        kernel,
        out_shape=(jax.ShapeDtypeStruct((2, 16), F32), jax.ShapeDtypeStruct((1, 2), F32)),
        in_specs=[pl.BlockSpec(memory_space=pl.ANY)] * 7,
        out_specs=(pl.BlockSpec(memory_space=pltpu.VMEM),) * 2,
        scratch_shapes=[
            vm((8, FG, JB), BF),
            vm((2 * NR, FG), BF),
            vm((FG, 128), BF),
            vm((128, FG), BF),
            vm((8, NR, JB), F32),
            vm((8, NR, JB), F32),
            vm((8, NR, JB), F32),
            vm((4, NR, JB), BF),
            vm((3, NR, JB), BF),
            vm((4, NR, JB), BF),
            vm((3, NR, JB), BF),
            vm((16, NR, JB), BF),
            vm((16, NQ, JB), BF),
            vm((16, NR, 2 * FA), BF),
            vm((2 * FA, IB), BF),
            vm((JB, IB), BF),
            vm((JB, IB), F32),
            vm((8, 2, NR, IB), F32),
            vm((KINDS, 4, 2 * NQ, IB), F32),
            vm((KINDS, 3, 2 * NQ, IB), F32),
            vm((KINDS, 4, 2 * NQ, IB), F32),
            vm((KINDS, 3, 2 * NQ, IB), F32),
            vm((16, NR, IB), BF),
            vm((16, NQ, IB), BF),
            vm((16, JB, IB), BF),
            vm((16, 24, 128), F32),
            vm((16, 24, 128), F32),
            vm((8, 8, 128), F32),
            vm((8, 128), F32),
            vm((2, 8, 128), F32),
            dma((7,)), dma((8,)), dma((4,)), dma((4,)), dma((8,)), dma((8,)),
            dma((4, CUTS)), dma((4, CUTS)), dma((3, CUTS)), dma((3, CUTS)),
            dma((KINDS, 4)), dma((KINDS, 4)), dma((KINDS, 3)), dma((KINDS, 3)),
            dma((15,)), dma((16,)), dma((15,)), dma((16,)), dma((16,)), dma((16,)),
            dma((7 * KINDS,)), dma((8, KINDS)), dma((8,)), dma((8,)),
            dma((16,)), dma((16,)), dma((8,)), dma((8,)), dma, dma,
        ],
        compiler_params=pltpu.CompilerParams(
            collective_id=0, has_side_effects=True, vmem_limit_bytes=56 * 1024 * 1024
        ),
        cost_estimate=pl.CostEstimate(flops=10_000_000_000, bytes_accessed=8_000_000, transcendentals=0),
    )(train_acts, query_acts, train_grads.T, query_grads, basis_in, basis_out, eigvals.T)
    return (scores.T * (1.0 / math.sqrt(D * H)), energies.reshape(2) / (D * H))


def solution(mesh):
    return jax.shard_map(
        on_device,
        mesh=mesh,
        in_specs=(
            P("dp", "mp"),
            P("dp", "mp"),
            P("dp", "mp"),
            P("dp", "mp"),
            P("mp", None),
            P("mp", None),
            P(None, "mp"),
        ),
        out_specs=(P(None, "dp"), P("dp")),
        check_vma=False,
    )
```

```python
import math

import jax
import jax.numpy as jnp
from jax import lax
from jax.experimental import pallas as pl
from jax.experimental.pallas import tpu as pltpu
from jax.sharding import PartitionSpec as P

D = 4096
H = 7168
SEQ = 64
DAMPING = 0.1
IB = 256
JB = 896
FG = 448
FA = 256
NQ = 32
NT = 64
NR = NQ + NT
CUTS = 3
KINDS = NR // NQ
CUT = NR // CUTS
BF = jnp.bfloat16
F32 = jnp.float32
MESH = pl.DeviceIdType.MESH


def dot(a, b):
    return jnp.dot(a, b, preferred_element_type=F32)


def kernel(
    ta_hbm, qa_hbm, tgt_hbm, qg_hbm, bi_hbm, bo_hbm, eig_hbm, sc_ref, en_ref,
    B, XG, TGT, TGS, PART, SIBS, SIBR, GPS, GSS, GPR, GSR, G96, QGS,
    ACT, BI, EIG, INV, APART, APS, ASS, APR, ASR, RA, QAS, S, MSG, R1, R2, X2, R3,
    load_sem, b_sem, swap_send, swap_recv, sib_send, sib_recv,
    gp_send, gp_recv, gs_send, gs_recv, ap_send, ap_recv, as_send, as_recv,
    xa_send, xa_recv, xg_send, xg_recv, qg_send, qg_recv, za_send, za_recv, qa_send, qa_recv,
    r1_send, r1_recv, r2_send, r2_recv, r3_send, r3_recv,
):
    d = lax.axis_index("dp")
    m = lax.axis_index("mp")
    z = m // 2
    c = m % 2
    s = 1 - 2 * c
    o = 1 - c
    su = 4 - 3 * c
    sv = 1 + 3 * c
    u = (d // su) % 4
    v = (d // sv) % 4
    sib = (d, 2 * z + o)

    def zat(delta):
        return (z + delta + 8) % 8

    def zdev(delta):
        return (d, 2 * zat(delta) + c)

    def slot_at(du, dv):
        return ((u + du + 4) % 4) * su + ((v + dv + 4) % 4) * sv

    def dpdev(du, dv):
        return (slot_at(du, dv), m)

    def remote(src, dst, send, recv, dev):
        return pltpu.make_async_remote_copy(
            src_ref=src, dst_ref=dst, send_sem=send, recv_sem=recv, device_id=dev, device_id_type=MESH
        )

    sends = []

    def push(src, dst, send, recv, dev):
        copy = remote(src, dst, send, recv, dev)
        copy.start()
        sends.append(copy)

    def arrived(dst, recv):
        remote(dst, dst, recv, recv, sib).wait_recv()

    barrier = pltpu.get_barrier_semaphore()
    greeted = [sib, zdev(1), zdev(-1)] + [dpdev(k, 0) for k in (1, 2, 3)] + [dpdev(0, k) for k in (1, 2, 3)]
    for dev in greeted:
        pl.semaphore_signal(barrier, inc=1, device_id=dev, device_id_type=MESH)

    def zoff(k):
        h = (k + 1) // 2
        return (4 - h) * (2 * (k % 2) - 1)

    def target(k):
        return (z + zoff(k) + 8) % 8

    loads = []

    def load(src, dst, sem):
        copy = pltpu.make_async_copy(src, dst, sem)
        copy.start()
        loads.append(copy)
        return copy

    own_cols = pl.ds(pl.multiple_of(c * FA, FA), FA)
    i_cols = pl.ds(pl.multiple_of(d * IB, IB), IB)

    def rows(cls, size):
        return pl.ds(pl.multiple_of(cls * size, size), size)

    l_tgt = load(tgt_hbm, TGT, load_sem.at[0])
    l_qg0 = load(qg_hbm.at[rows(c, NQ)], XG.at[pl.ds(0, NQ)], load_sem.at[1])
    l_qg1 = load(qg_hbm.at[rows(o, NQ)], XG.at[pl.ds(NR, NQ)], load_sem.at[2])
    b_loads = []
    for k in range(8):
        col = pl.multiple_of(target(k) * JB, 128)
        b_loads.append(load(bo_hbm.at[:, pl.ds(col, JB)], B.at[k], b_sem.at[k]))
    l_ta = load(ta_hbm.at[rows(c, NT)], ACT.at[d, pl.ds(NQ, NT), own_cols], load_sem.at[3])
    l_qa = load(qa_hbm.at[rows(c, NQ)], ACT.at[d, pl.ds(0, NQ), own_cols], load_sem.at[4])
    l_bi = load(bi_hbm.at[:, i_cols], BI.at[own_cols], load_sem.at[5])
    eig_rows = pl.ds(pl.multiple_of(c * FG, FG), FG)
    l_eig = load(eig_hbm.at[:, i_cols], EIG.at[eig_rows], load_sem.at[6])

    sib_cols = pl.ds(pl.multiple_of(o * FA, FA), FA)

    l_tgt.wait()
    TGS[...] = jnp.transpose(TGT[...].astype(F32)).astype(BF)
    XG[pl.ds(NQ, NT), :] = TGS[rows(c, NT), :]
    XG[pl.ds(NR + NQ, NT), :] = TGS[rows(o, NT), :]
    l_qg0.wait()
    l_qg1.wait()

    def swap_inputs():
        push(ta_hbm.at[rows(o, NT)], ACT.at[d, pl.ds(NQ, NT), own_cols], swap_send.at[0], swap_recv.at[0], sib)
        push(qa_hbm.at[rows(o, NQ)], ACT.at[d, pl.ds(0, NQ), own_cols], swap_send.at[1], swap_recv.at[1], sib)
        push(bi_hbm.at[:, i_cols], BI.at[own_cols], swap_send.at[2], swap_recv.at[2], sib)
        push(eig_hbm.at[:, i_cols], EIG.at[eig_rows], swap_send.at[3], swap_recv.at[3], sib)

    def g_partial(k):
        b_loads[k].wait()
        part = dot(XG[...], B[k])
        PART[k] = part[:NR]
        SIBS[k] = part[NR:]

    def g_swap(k):
        push(SIBS.at[k], SIBR.at[k], sib_send.at[k], sib_recv.at[k], sib)

    def make_gather(buf, send, recv, landed):
        count = [0]

        def go(slot, dev):
            push(buf.at[slot], buf.at[slot], send.at[count[0]], recv.at[slot], dev)
            count[0] += 1

        def along_v(du):
            for dv in (1, 3, 2):
                go(slot_at(du, 0), dpdev(0, dv))

        def start():
            for du in (1, 3, 2):
                go(slot_at(0, 0), dpdev(du, 0))
            along_v(0)
            landed(slot_at(0, 0))

        def got(du, dv):
            slot = slot_at(du, dv)
            arrived(buf.at[slot], recv.at[slot])
            if dv == 0:
                along_v(du)
            landed(slot)

        return start, got

    def g_query_to_sibling(slot):
        push(G96.at[slot, pl.ds(0, NQ)], QGS.at[slot], qg_send.at[slot], qg_recv.at[slot], sib)

    xa_start, xa_got = make_gather(ACT, xa_send, xa_recv, lambda slot: None)
    xg_start, xg_got = make_gather(G96, xg_send, xg_recv, g_query_to_sibling)

    def g_own(k, h):
        part = pl.ds(h * CUT, CUT)
        return PART[k, part, :] + SIBR[k, part, :]

    def g_ring(step):
        kp = 0 if step == 0 else 2 * step - 1 + c
        arrived(SIBR.at[kp], sib_recv.at[kp])
        if step < 3:
            ks = 2 * (step + 1) - c
            arrived(SIBR.at[ks], sib_recv.at[ks])
        for h in range(CUTS):
            part = pl.ds(h * CUT, CUT)
            total = g_own(kp, h)
            if step > 0:
                arrived(GPR.at[step - 1, part], gp_recv.at[step - 1, h])
                total = total + GPR[step - 1, part, :].astype(F32)
            GPS[step, part, :] = total.astype(BF)
            push(GPS.at[step, part], GPR.at[step, part], gp_send.at[step, h], gp_recv.at[step, h], zdev(s))
            if step < 3:
                total = g_own(ks, h)
                if step > 0:
                    arrived(GSR.at[step - 1, part], gs_recv.at[step - 1, h])
                    total = total + GSR[step - 1, part, :].astype(F32)
                GSS[step, part, :] = total.astype(BF)
                push(GSS.at[step, part], GSR.at[step, part], gs_send.at[step, h], gs_recv.at[step, h], zdev(-s))

    def g_final():
        arrived(SIBR.at[7], sib_recv.at[7])
        for h in range(CUTS):
            part = pl.ds(h * CUT, CUT)
            total = g_own(7, h)
            arrived(GSR.at[2, part], gs_recv.at[2, h])
            total = total + GSR[2, part, :].astype(F32)
            arrived(GPR.at[3, part], gp_recv.at[3, h])
            total = total + GPR[3, part, :].astype(F32)
            G96[d, part, :] = total.astype(BF)

    kind_rows = tuple(pl.ds(k * NQ, NQ) for k in range(KINDS))

    def a_local(delta):
        block = zat(delta)
        both = dot(ACT[pl.ds(2 * block, 2)].reshape(2 * NR, 2 * FA), BI[...])
        APART[block] = both.reshape(2, NR, IB)

    def a_own(delta, kind):
        return APART[zat(delta), :, kind_rows[kind], :].reshape(2 * NQ, IB)

    def a_step(i):
        if i == 0:
            a_local(4 * s)
            a_local(-3 * s)
        for kind in range(KINDS):
            total = a_own(s * (4 - i), kind)
            if i > 0:
                arrived(APR.at[kind, i - 1], ap_recv.at[kind, i - 1])
                total = total + APR[kind, i - 1]
            APS[kind, i] = total
            push(APS.at[kind, i], APR.at[kind, i], ap_send.at[kind, i], ap_recv.at[kind, i], zdev(s))
            if i < 3:
                total = a_own(-s * (3 - i), kind)
                if i > 0:
                    arrived(ASR.at[kind, i - 1], as_recv.at[kind, i - 1])
                    total = total + ASR[kind, i - 1]
                ASS[kind, i] = total
                push(ASS.at[kind, i], ASR.at[kind, i], as_send.at[kind, i], as_recv.at[kind, i], zdev(-s))
        if i == 0:
            for delta in (3 * s, -2 * s, 2 * s, -s, s, 0):
                a_local(delta)

    def a_final(kind):
        total = a_own(0, kind)
        arrived(ASR.at[kind, 2], as_recv.at[kind, 2])
        total = total + ASR[kind, 2]
        arrived(APR.at[kind, 3], ap_recv.at[kind, 3])
        total = total + APR[kind, 3]
        RA[pl.ds(2 * z, 2), kind_rows[kind], :] = total.astype(BF).reshape(2, NQ, IB)

    def za_ref(delta, kind):
        block = (z + delta + 8) % 8
        return RA.at[pl.ds(2 * block, 2), kind_rows[kind]]

    def za_index(delta):
        return (z + delta + 8) % 8

    za_count = [0]

    def za_go(delta, kind, dev):
        ref = za_ref(delta, kind)
        push(ref, ref, za_send.at[za_count[0]], za_recv.at[za_index(delta), kind], dev)
        za_count[0] += 1

    def za_got(delta, kind):
        arrived(za_ref(delta, kind), za_recv.at[za_index(delta), kind])

    def za_share(delta):
        block = za_index(delta)
        push(za_ref(delta, 0), QAS.at[pl.ds(2 * block, 2)], qa_send.at[block], qa_recv.at[block], sib)

    def za_start(kind):
        for delta in (2, -2, 1, -1):
            za_go(0, kind, zdev(delta))
        if kind == 0:
            za_share(0)

    def za_far(kind):
        za_got(-2 * s, kind)
        za_go(-2 * s, kind, zdev(2 * s))
        za_go(-2 * s, kind, zdev(s))
        za_got(2 * s, kind)
        za_go(2 * s, kind, zdev(-s))
        if kind == 0:
            za_share(-2 * s)
            za_share(2 * s)

    def za_take(deltas, kind):
        for delta in deltas:
            za_got(delta, kind)
            if kind == 0:
                za_share(delta)

    def nth_slot(p):
        k = p // 2
        return 2 * zat(((k + 1) // 2) * (2 * (k % 2) - 1)) + p % 2

    def outers(first, last):
        def one(p, carry):
            slot = nth_slot(p)
            acts = RA[slot, pl.ds(NQ, NT), :]
            energy = jnp.zeros((8, 128), F32)
            for j in range(JB // 128):
                cols = pl.ds(j * 128, 128)
                outer = lax.dot_general(
                    G96[slot, pl.ds(NQ, NT), cols], acts, (((0,), (0,)), ((), ())), preferred_element_type=F32
                )
                square = outer * outer
                energy = energy + jnp.sum((square[:, :128] + square[:, 128:]).reshape(16, 8, 128), axis=0)
                S[slot, cols, :] = (outer * INV[cols, :]).astype(BF)
            MSG[slot, pl.ds(16, 8), :] = energy
            return carry

        lax.fori_loop(first, last, one, 0)

    def scores_of(slot):
        total = jnp.zeros((16, 8, 128), F32)
        for cls in range(2):
            grads = G96[:, pl.ds(0, NQ), :] if cls == 0 else QGS[...]
            acts = RA[:, pl.ds(0, NQ), :] if cls == 0 else QAS[...]
            applied = dot(grads.reshape(16 * NQ, JB), S[slot]) * acts.reshape(16 * NQ, IB).astype(F32)
            total = total + jnp.sum((applied[:, :128] + applied[:, 128:]).reshape(16, NQ // 8, 8, 128), axis=1)
        MSG[slot, pl.ds(0, 16), :] = jnp.sum(total, axis=1)

    def r1_copy(peer):
        return remote(MSG.at[peer], R1.at[d], r1_send.at[peer], r1_recv.at[d], (peer, m))

    def scores(first, last):
        def one(p, carry):
            slot = nth_slot(p)
            scores_of(slot)

            @pl.when(slot != d)
            def _():
                r1_copy(slot).start()

            @pl.when(slot == d)
            def _():
                R1[d] = MSG[d]

            return carry

        lax.fori_loop(first, last, one, 0)

    for k in (0, 1, 2):
        g_partial(k)
    pl.semaphore_wait(barrier, len(greeted))
    swap_inputs()
    for k in (0, 1, 2):
        g_swap(k)
    l_ta.wait()
    l_qa.wait()
    arrived(ACT.at[d, pl.ds(NQ, NT), sib_cols], swap_recv.at[0])
    arrived(ACT.at[d, pl.ds(0, NQ), sib_cols], swap_recv.at[1])
    xa_start()
    g_ring(0)
    for k in range(3, 8):
        g_partial(k)
        g_swap(k)
    g_ring(1)
    xa_got(1, 0)
    xa_got(3, 0)
    l_bi.wait()
    l_eig.wait()
    sib_eig = pl.ds(pl.multiple_of(o * FG, FG), FG)
    arrived(BI.at[sib_cols], swap_recv.at[2])
    arrived(EIG.at[sib_eig], swap_recv.at[3])
    INV[...] = 1.0 / (EIG[...].astype(F32) + DAMPING)
    xa_got(2, 0)
    g_ring(2)
    for du in (0, 1, 3, 2):
        if du == 2:
            g_ring(3)
        for dv in (1, 3, 2):
            xa_got(du, dv)
    a_step(0)
    g_final()
    xg_start()
    a_step(1)
    xg_got(1, 0)
    xg_got(3, 0)
    xg_got(2, 0)
    a_step(2)
    for dv in (1, 3, 2):
        xg_got(0, dv)
    a_step(3)
    for kind in range(KINDS):
        a_final(kind)
        za_start(kind)
    for du in (1, 3):
        for dv in (1, 3, 2):
            xg_got(du, dv)
    za_far(0)
    for dv in (1, 3, 2):
        xg_got(2, dv)
    outers(0, 2)
    za_take((1, -1), 0)
    za_far(1)
    za_far(2)
    for kind in (1, 2):
        za_take((1, -1), kind)
    outers(2, 10)
    za_take((3, -3, 4), 0)
    for k in range(16):
        arrived(QGS.at[k], qg_recv.at[k])
    for k in range(8):
        arrived(QAS.at[pl.ds(2 * k, 2)], qa_recv.at[k])
    scores(0, 10)
    for kind in (1, 2):
        za_take((3, -3, 4), kind)
    outers(10, 16)
    scores(10, 16)
    for k in range(1, 16):
        peer = (d + k) % 16
        arrived(R1.at[peer], r1_recv.at[peer])

    def over_lanes(x):
        return lax.dot_general(
            jnp.ones((8, 128), F32), x, (((1,), (1,)), ((), ())), precision=lax.Precision.HIGHEST,
            preferred_element_type=F32,
        )

    X2[...] = jnp.zeros((8, 128), F32)
    X2[:, pl.ds(0, 24)] = over_lanes(jnp.sum(R1[...], axis=0))
    R2[z] = X2[...]
    for delta in (4, 3, -3, 2, -2, 1, -1):
        push(X2, R2.at[z], r2_send.at[delta + 3], r2_recv.at[z], zdev(delta))
    for delta in (1, -1, 2, -2, 3, -3, 4):
        arrived(R2.at[zat(delta)], r2_recv.at[zat(delta)])
    R3[c] = jnp.sum(R2[...], axis=0)
    push(R3.at[c], R3.at[c], r3_send, r3_recv, sib)
    arrived(R3.at[o], r3_recv)
    for cls in range(2):
        sc_ref[pl.ds(cls, 1), :] = R3[cls, :1, :16]
        en_ref[:, pl.ds(cls, 1)] = jnp.sum(R3[cls, :1, 16:24], axis=1, keepdims=True)
    for copy in sends:
        copy.wait_send()
    for k in range(1, 16):
        r1_copy((d + k) % 16).wait_send()


def on_device(train_acts, train_grads, query_acts, query_grads, basis_in, basis_out, eigvals):
    dma = pltpu.SemaphoreType.DMA
    vm = pltpu.VMEM
    scores, energies = pl.pallas_call(
        kernel,
        out_shape=(jax.ShapeDtypeStruct((2, 16), F32), jax.ShapeDtypeStruct((1, 2), F32)),
        in_specs=[pl.BlockSpec(memory_space=pl.ANY)] * 7,
        out_specs=(pl.BlockSpec(memory_space=pltpu.VMEM),) * 2,
        scratch_shapes=[
            vm((8, FG, JB), BF),
            vm((2 * NR, FG), BF),
            vm((FG, 128), BF),
            vm((128, FG), BF),
            vm((8, NR, JB), F32),
            vm((8, NR, JB), F32),
            vm((8, NR, JB), F32),
            vm((4, NR, JB), BF),
            vm((3, NR, JB), BF),
            vm((4, NR, JB), BF),
            vm((3, NR, JB), BF),
            vm((16, NR, JB), BF),
            vm((16, NQ, JB), BF),
            vm((16, NR, 2 * FA), BF),
            vm((2 * FA, IB), BF),
            vm((JB, IB), BF),
            vm((JB, IB), F32),
            vm((8, 2, NR, IB), F32),
            vm((KINDS, 4, 2 * NQ, IB), F32),
            vm((KINDS, 3, 2 * NQ, IB), F32),
            vm((KINDS, 4, 2 * NQ, IB), F32),
            vm((KINDS, 3, 2 * NQ, IB), F32),
            vm((16, NR, IB), BF),
            vm((16, NQ, IB), BF),
            vm((16, JB, IB), BF),
            vm((16, 24, 128), F32),
            vm((16, 24, 128), F32),
            vm((8, 8, 128), F32),
            vm((8, 128), F32),
            vm((2, 8, 128), F32),
            dma((7,)), dma((8,)), dma((4,)), dma((4,)), dma((8,)), dma((8,)),
            dma((4, CUTS)), dma((4, CUTS)), dma((3, CUTS)), dma((3, CUTS)),
            dma((KINDS, 4)), dma((KINDS, 4)), dma((KINDS, 3)), dma((KINDS, 3)),
            dma((15,)), dma((16,)), dma((15,)), dma((16,)), dma((16,)), dma((16,)),
            dma((7 * KINDS,)), dma((8, KINDS)), dma((8,)), dma((8,)),
            dma((16,)), dma((16,)), dma((8,)), dma((8,)), dma, dma,
        ],
        compiler_params=pltpu.CompilerParams(
            collective_id=0, has_side_effects=True, vmem_limit_bytes=56 * 1024 * 1024
        ),
        cost_estimate=pl.CostEstimate(flops=10_000_000_000, bytes_accessed=8_000_000, transcendentals=0),
    )(train_acts, query_acts, train_grads.T, query_grads, basis_in, basis_out, eigvals.T)
    return (scores.T * (1.0 / math.sqrt(D * H)), energies.reshape(2) / (D * H))


def solution(mesh):
    return jax.shard_map(
        on_device,
        mesh=mesh,
        in_specs=(
            P("dp", "mp"),
            P("dp", "mp"),
            P("dp", "mp"),
            P("dp", "mp"),
            P("mp", None),
            P("mp", None),
            P(None, "mp"),
        ),
        out_specs=(P(None, "dp"), P("dp")),
        check_vma=False,
    )
```

```python
import math

import jax
import jax.numpy as jnp
from jax import lax
from jax.experimental import pallas as pl
from jax.experimental.pallas import tpu as pltpu
from jax.sharding import PartitionSpec as P

D = 4096
H = 7168
SEQ = 64
DAMPING = 0.1
IB = 256
JB = 896
FG = 448
FA = 256
NQ = 32
NT = 64
NR = NQ + NT
CUTS = 3
KINDS = NR // NQ
CUT = NR // CUTS
BF = jnp.bfloat16
F32 = jnp.float32
MESH = pl.DeviceIdType.MESH


def dot(a, b):
    return jnp.dot(a, b, preferred_element_type=F32)


def kernel(
    ta_hbm, qa_hbm, tgt_hbm, qg_hbm, bi_hbm, bo_hbm, eig_hbm, sc_ref, en_ref,
    B, XG, TGT, TGS, PART, SIBS, SIBR, GPS, GSS, GPR, GSR, G96, QGS,
    ACT, BI, EIG, INV, APART, APS, ASS, APR, ASR, RA, QAS, S, MSG, R1, R2, X2, R3,
    load_sem, b_sem, swap_send, swap_recv, sib_send, sib_recv,
    gp_send, gp_recv, gs_send, gs_recv, ap_send, ap_recv, as_send, as_recv,
    xa_send, xa_recv, xg_send, xg_recv, qg_send, qg_recv, za_send, za_recv, qa_send, qa_recv,
    r1_send, r1_recv, r2_send, r2_recv, r3_send, r3_recv,
):
    d = lax.axis_index("dp")
    m = lax.axis_index("mp")
    z = m // 2
    c = m % 2
    s = 1 - 2 * c
    o = 1 - c
    su = 4 - 3 * c
    sv = 1 + 3 * c
    u = (d // su) % 4
    v = (d // sv) % 4
    sib = (d, 2 * z + o)

    def zat(delta):
        return (z + delta + 8) % 8

    def zdev(delta):
        return (d, 2 * zat(delta) + c)

    def slot_at(du, dv):
        return ((u + du + 4) % 4) * su + ((v + dv + 4) % 4) * sv

    def dpdev(du, dv):
        return (slot_at(du, dv), m)

    def remote(src, dst, send, recv, dev):
        return pltpu.make_async_remote_copy(
            src_ref=src, dst_ref=dst, send_sem=send, recv_sem=recv, device_id=dev, device_id_type=MESH
        )

    sends = []

    def push(src, dst, send, recv, dev):
        copy = remote(src, dst, send, recv, dev)
        copy.start()
        sends.append(copy)

    def arrived(dst, recv):
        remote(dst, dst, recv, recv, sib).wait_recv()

    barrier = pltpu.get_barrier_semaphore()
    greeted = [sib, zdev(1), zdev(-1)] + [dpdev(k, 0) for k in (1, 2, 3)] + [dpdev(0, k) for k in (1, 2, 3)]
    for dev in greeted:
        pl.semaphore_signal(barrier, inc=1, device_id=dev, device_id_type=MESH)

    def zoff(k):
        h = (k + 1) // 2
        return (4 - h) * (2 * (k % 2) - 1)

    def target(k):
        return (z + zoff(k) + 8) % 8

    loads = []

    def load(src, dst, sem):
        copy = pltpu.make_async_copy(src, dst, sem)
        copy.start()
        loads.append(copy)
        return copy

    own_cols = pl.ds(pl.multiple_of(c * FA, FA), FA)
    i_cols = pl.ds(pl.multiple_of(d * IB, IB), IB)

    def rows(cls, size):
        return pl.ds(pl.multiple_of(cls * size, size), size)

    l_tgt = load(tgt_hbm, TGT, load_sem.at[0])
    l_qg0 = load(qg_hbm.at[rows(c, NQ)], XG.at[pl.ds(0, NQ)], load_sem.at[1])
    l_qg1 = load(qg_hbm.at[rows(o, NQ)], XG.at[pl.ds(NR, NQ)], load_sem.at[2])
    b_loads = []
    for k in range(8):
        col = pl.multiple_of(target(k) * JB, 128)
        b_loads.append(load(bo_hbm.at[:, pl.ds(col, JB)], B.at[k], b_sem.at[k]))
    l_ta = load(ta_hbm.at[rows(c, NT)], ACT.at[d, pl.ds(NQ, NT), own_cols], load_sem.at[3])
    l_qa = load(qa_hbm.at[rows(c, NQ)], ACT.at[d, pl.ds(0, NQ), own_cols], load_sem.at[4])
    l_bi = load(bi_hbm.at[:, i_cols], BI.at[own_cols], load_sem.at[5])
    eig_rows = pl.ds(pl.multiple_of(c * FG, FG), FG)
    l_eig = load(eig_hbm.at[:, i_cols], EIG.at[eig_rows], load_sem.at[6])

    sib_cols = pl.ds(pl.multiple_of(o * FA, FA), FA)

    l_tgt.wait()
    TGS[...] = jnp.transpose(TGT[...].astype(F32)).astype(BF)
    XG[pl.ds(NQ, NT), :] = TGS[rows(c, NT), :]
    XG[pl.ds(NR + NQ, NT), :] = TGS[rows(o, NT), :]
    l_qg0.wait()
    l_qg1.wait()

    def swap_inputs():
        push(ta_hbm.at[rows(o, NT)], ACT.at[d, pl.ds(NQ, NT), own_cols], swap_send.at[0], swap_recv.at[0], sib)
        push(qa_hbm.at[rows(o, NQ)], ACT.at[d, pl.ds(0, NQ), own_cols], swap_send.at[1], swap_recv.at[1], sib)
        push(bi_hbm.at[:, i_cols], BI.at[own_cols], swap_send.at[2], swap_recv.at[2], sib)
        push(eig_hbm.at[:, i_cols], EIG.at[eig_rows], swap_send.at[3], swap_recv.at[3], sib)

    def g_partial(k):
        b_loads[k].wait()
        part = dot(XG[...], B[k])
        PART[k] = part[:NR]
        SIBS[k] = part[NR:]

    def g_swap(k):
        push(SIBS.at[k], SIBR.at[k], sib_send.at[k], sib_recv.at[k], sib)

    def make_gather(buf, send, recv, landed):
        count = [0]

        def go(slot, dev):
            push(buf.at[slot], buf.at[slot], send.at[count[0]], recv.at[slot], dev)
            count[0] += 1

        def along_v(du):
            for dv in (1, 3, 2):
                go(slot_at(du, 0), dpdev(0, dv))

        def start():
            for du in (1, 3, 2):
                go(slot_at(0, 0), dpdev(du, 0))
            along_v(0)
            landed(slot_at(0, 0))

        def got(du, dv):
            slot = slot_at(du, dv)
            arrived(buf.at[slot], recv.at[slot])
            if dv == 0:
                along_v(du)
            landed(slot)

        return start, got

    def g_query_to_sibling(slot):
        push(G96.at[slot, pl.ds(0, NQ)], QGS.at[slot], qg_send.at[slot], qg_recv.at[slot], sib)

    xa_start, xa_got = make_gather(ACT, xa_send, xa_recv, lambda slot: None)
    xg_start, xg_got = make_gather(G96, xg_send, xg_recv, g_query_to_sibling)

    def g_own(k, h):
        part = pl.ds(h * CUT, CUT)
        return PART[k, part, :] + SIBR[k, part, :]

    def g_ring(step):
        kp = 0 if step == 0 else 2 * step - 1 + c
        arrived(SIBR.at[kp], sib_recv.at[kp])
        if step < 3:
            ks = 2 * (step + 1) - c
            arrived(SIBR.at[ks], sib_recv.at[ks])
        for h in range(CUTS):
            part = pl.ds(h * CUT, CUT)
            total = g_own(kp, h)
            if step > 0:
                arrived(GPR.at[step - 1, part], gp_recv.at[step - 1, h])
                total = total + GPR[step - 1, part, :].astype(F32)
            GPS[step, part, :] = total.astype(BF)
            push(GPS.at[step, part], GPR.at[step, part], gp_send.at[step, h], gp_recv.at[step, h], zdev(s))
            if step < 3:
                total = g_own(ks, h)
                if step > 0:
                    arrived(GSR.at[step - 1, part], gs_recv.at[step - 1, h])
                    total = total + GSR[step - 1, part, :].astype(F32)
                GSS[step, part, :] = total.astype(BF)
                push(GSS.at[step, part], GSR.at[step, part], gs_send.at[step, h], gs_recv.at[step, h], zdev(-s))

    def g_final():
        arrived(SIBR.at[7], sib_recv.at[7])
        for h in range(CUTS):
            part = pl.ds(h * CUT, CUT)
            total = g_own(7, h)
            arrived(GSR.at[2, part], gs_recv.at[2, h])
            total = total + GSR[2, part, :].astype(F32)
            arrived(GPR.at[3, part], gp_recv.at[3, h])
            total = total + GPR[3, part, :].astype(F32)
            G96[d, part, :] = total.astype(BF)

    kind_rows = tuple(pl.ds(k * NQ, NQ) for k in range(KINDS))

    def a_local(delta):
        block = zat(delta)
        both = dot(ACT[pl.ds(2 * block, 2)].reshape(2 * NR, 2 * FA), BI[...])
        APART[block] = both.reshape(2, NR, IB)

    def a_own(delta, kind):
        return APART[zat(delta), :, kind_rows[kind], :].reshape(2 * NQ, IB)

    def a_step(i):
        if i == 0:
            a_local(4 * s)
            a_local(-3 * s)
        for kind in range(KINDS):
            total = a_own(s * (4 - i), kind)
            if i > 0:
                arrived(APR.at[kind, i - 1], ap_recv.at[kind, i - 1])
                total = total + APR[kind, i - 1]
            APS[kind, i] = total
            push(APS.at[kind, i], APR.at[kind, i], ap_send.at[kind, i], ap_recv.at[kind, i], zdev(s))
            if i < 3:
                total = a_own(-s * (3 - i), kind)
                if i > 0:
                    arrived(ASR.at[kind, i - 1], as_recv.at[kind, i - 1])
                    total = total + ASR[kind, i - 1]
                ASS[kind, i] = total
                push(ASS.at[kind, i], ASR.at[kind, i], as_send.at[kind, i], as_recv.at[kind, i], zdev(-s))

    def a_locals():
        for delta in (3 * s, -2 * s, 2 * s, -s, s, 0):
            a_local(delta)

    def a_final(kind):
        total = a_own(0, kind)
        arrived(ASR.at[kind, 2], as_recv.at[kind, 2])
        total = total + ASR[kind, 2]
        arrived(APR.at[kind, 3], ap_recv.at[kind, 3])
        total = total + APR[kind, 3]
        RA[pl.ds(2 * z, 2), kind_rows[kind], :] = total.astype(BF).reshape(2, NQ, IB)

    def za_ref(delta, kind):
        block = (z + delta + 8) % 8
        return RA.at[pl.ds(2 * block, 2), kind_rows[kind]]

    def za_index(delta):
        return (z + delta + 8) % 8

    za_count = [0]

    def za_go(delta, kind, dev):
        ref = za_ref(delta, kind)
        push(ref, ref, za_send.at[za_count[0]], za_recv.at[za_index(delta), kind], dev)
        za_count[0] += 1

    def za_got(delta, kind):
        arrived(za_ref(delta, kind), za_recv.at[za_index(delta), kind])

    def za_share(delta):
        block = za_index(delta)
        push(za_ref(delta, 0), QAS.at[pl.ds(2 * block, 2)], qa_send.at[block], qa_recv.at[block], sib)

    def za_start(kind):
        for delta in (2, -2, 1, -1):
            za_go(0, kind, zdev(delta))
        if kind == 0:
            za_share(0)

    def za_far(kind):
        za_got(-2 * s, kind)
        za_go(-2 * s, kind, zdev(2 * s))
        za_go(-2 * s, kind, zdev(s))
        za_got(2 * s, kind)
        za_go(2 * s, kind, zdev(-s))
        if kind == 0:
            za_share(-2 * s)
            za_share(2 * s)

    def za_take(deltas, kind):
        for delta in deltas:
            za_got(delta, kind)
            if kind == 0:
                za_share(delta)

    def nth_slot(p):
        k = p // 2
        return 2 * zat(((k + 1) // 2) * (2 * (k % 2) - 1)) + p % 2

    def outers(first, last):
        def one(p, carry):
            slot = nth_slot(p)
            acts = RA[slot, pl.ds(NQ, NT), :]
            energy = jnp.zeros((8, 128), F32)
            for j in range(JB // 128):
                cols = pl.ds(j * 128, 128)
                outer = lax.dot_general(
                    G96[slot, pl.ds(NQ, NT), cols], acts, (((0,), (0,)), ((), ())), preferred_element_type=F32
                )
                square = outer * outer
                energy = energy + jnp.sum((square[:, :128] + square[:, 128:]).reshape(16, 8, 128), axis=0)
                S[slot, cols, :] = (outer * INV[cols, :]).astype(BF)
            MSG[slot, pl.ds(16, 8), :] = energy
            return carry

        lax.fori_loop(first, last, one, 0)

    def scores_of(slot):
        total = jnp.zeros((16, 8, 128), F32)
        for cls in range(2):
            grads = G96[:, pl.ds(0, NQ), :] if cls == 0 else QGS[...]
            acts = RA[:, pl.ds(0, NQ), :] if cls == 0 else QAS[...]
            applied = dot(grads.reshape(16 * NQ, JB), S[slot]) * acts.reshape(16 * NQ, IB).astype(F32)
            total = total + jnp.sum((applied[:, :128] + applied[:, 128:]).reshape(16, NQ // 8, 8, 128), axis=1)
        MSG[slot, pl.ds(0, 16), :] = jnp.sum(total, axis=1)

    def r1_copy(peer):
        return remote(MSG.at[peer], R1.at[d], r1_send.at[peer], r1_recv.at[d], (peer, m))

    def scores(first, last):
        def one(p, carry):
            slot = nth_slot(p)
            scores_of(slot)

            @pl.when(slot != d)
            def _():
                r1_copy(slot).start()

            @pl.when(slot == d)
            def _():
                R1[d] = MSG[d]

            return carry

        lax.fori_loop(first, last, one, 0)

    for k in (0, 1, 2):
        g_partial(k)
    pl.semaphore_wait(barrier, len(greeted))
    swap_inputs()
    for k in (0, 1, 2):
        g_swap(k)
    l_ta.wait()
    l_qa.wait()
    arrived(ACT.at[d, pl.ds(NQ, NT), sib_cols], swap_recv.at[0])
    arrived(ACT.at[d, pl.ds(0, NQ), sib_cols], swap_recv.at[1])
    xa_start()
    g_ring(0)
    for k in range(3, 8):
        g_partial(k)
        g_swap(k)
    g_ring(1)
    xa_got(1, 0)
    xa_got(3, 0)
    l_bi.wait()
    l_eig.wait()
    sib_eig = pl.ds(pl.multiple_of(o * FG, FG), FG)
    arrived(BI.at[sib_cols], swap_recv.at[2])
    arrived(EIG.at[sib_eig], swap_recv.at[3])
    INV[...] = 1.0 / (EIG[...].astype(F32) + DAMPING)
    xa_got(2, 0)
    g_ring(2)
    for du in (0, 1, 3, 2):
        if du == 2:
            g_ring(3)
        for dv in (1, 3, 2):
            xa_got(du, dv)
    a_step(0)
    g_final()
    xg_start()
    a_locals()
    a_step(1)
    xg_got(1, 0)
    xg_got(3, 0)
    xg_got(2, 0)
    a_step(2)
    for dv in (1, 3, 2):
        xg_got(0, dv)
    a_step(3)
    for kind in range(KINDS):
        a_final(kind)
        za_start(kind)
    for du in (1, 3):
        for dv in (1, 3, 2):
            xg_got(du, dv)
    za_far(0)
    for dv in (1, 3, 2):
        xg_got(2, dv)
    outers(0, 2)
    za_take((1, -1), 0)
    za_far(1)
    za_far(2)
    for kind in (1, 2):
        za_take((1, -1), kind)
    outers(2, 10)
    za_take((3, -3, 4), 0)
    for k in range(16):
        arrived(QGS.at[k], qg_recv.at[k])
    for k in range(8):
        arrived(QAS.at[pl.ds(2 * k, 2)], qa_recv.at[k])
    scores(0, 10)
    for kind in (1, 2):
        za_take((3, -3, 4), kind)
    outers(10, 16)
    scores(10, 16)
    for k in range(1, 16):
        peer = (d + k) % 16
        arrived(R1.at[peer], r1_recv.at[peer])

    def over_lanes(x):
        return lax.dot_general(
            jnp.ones((8, 128), F32), x, (((1,), (1,)), ((), ())), precision=lax.Precision.HIGHEST,
            preferred_element_type=F32,
        )

    X2[...] = jnp.zeros((8, 128), F32)
    X2[:, pl.ds(0, 24)] = over_lanes(jnp.sum(R1[...], axis=0))
    R2[z] = X2[...]
    for delta in (4, 3, -3, 2, -2, 1, -1):
        push(X2, R2.at[z], r2_send.at[delta + 3], r2_recv.at[z], zdev(delta))
    for delta in (1, -1, 2, -2, 3, -3, 4):
        arrived(R2.at[zat(delta)], r2_recv.at[zat(delta)])
    R3[c] = jnp.sum(R2[...], axis=0)
    push(R3.at[c], R3.at[c], r3_send, r3_recv, sib)
    arrived(R3.at[o], r3_recv)
    for cls in range(2):
        sc_ref[pl.ds(cls, 1), :] = R3[cls, :1, :16]
        en_ref[:, pl.ds(cls, 1)] = jnp.sum(R3[cls, :1, 16:24], axis=1, keepdims=True)
    for copy in sends:
        copy.wait_send()
    for k in range(1, 16):
        r1_copy((d + k) % 16).wait_send()


def on_device(train_acts, train_grads, query_acts, query_grads, basis_in, basis_out, eigvals):
    dma = pltpu.SemaphoreType.DMA
    vm = pltpu.VMEM
    scores, energies = pl.pallas_call(
        kernel,
        out_shape=(jax.ShapeDtypeStruct((2, 16), F32), jax.ShapeDtypeStruct((1, 2), F32)),
        in_specs=[pl.BlockSpec(memory_space=pl.ANY)] * 7,
        out_specs=(pl.BlockSpec(memory_space=pltpu.VMEM),) * 2,
        scratch_shapes=[
            vm((8, FG, JB), BF),
            vm((2 * NR, FG), BF),
            vm((FG, 128), BF),
            vm((128, FG), BF),
            vm((8, NR, JB), F32),
            vm((8, NR, JB), F32),
            vm((8, NR, JB), F32),
            vm((4, NR, JB), BF),
            vm((3, NR, JB), BF),
            vm((4, NR, JB), BF),
            vm((3, NR, JB), BF),
            vm((16, NR, JB), BF),
            vm((16, NQ, JB), BF),
            vm((16, NR, 2 * FA), BF),
            vm((2 * FA, IB), BF),
            vm((JB, IB), BF),
            vm((JB, IB), F32),
            vm((8, 2, NR, IB), F32),
            vm((KINDS, 4, 2 * NQ, IB), F32),
            vm((KINDS, 3, 2 * NQ, IB), F32),
            vm((KINDS, 4, 2 * NQ, IB), F32),
            vm((KINDS, 3, 2 * NQ, IB), F32),
            vm((16, NR, IB), BF),
            vm((16, NQ, IB), BF),
            vm((16, JB, IB), BF),
            vm((16, 24, 128), F32),
            vm((16, 24, 128), F32),
            vm((8, 8, 128), F32),
            vm((8, 128), F32),
            vm((2, 8, 128), F32),
            dma((7,)), dma((8,)), dma((4,)), dma((4,)), dma((8,)), dma((8,)),
            dma((4, CUTS)), dma((4, CUTS)), dma((3, CUTS)), dma((3, CUTS)),
            dma((KINDS, 4)), dma((KINDS, 4)), dma((KINDS, 3)), dma((KINDS, 3)),
            dma((15,)), dma((16,)), dma((15,)), dma((16,)), dma((16,)), dma((16,)),
            dma((7 * KINDS,)), dma((8, KINDS)), dma((8,)), dma((8,)),
            dma((16,)), dma((16,)), dma((8,)), dma((8,)), dma, dma,
        ],
        compiler_params=pltpu.CompilerParams(
            collective_id=0, has_side_effects=True, vmem_limit_bytes=56 * 1024 * 1024
        ),
        cost_estimate=pl.CostEstimate(flops=10_000_000_000, bytes_accessed=8_000_000, transcendentals=0),
    )(train_acts, query_acts, train_grads.T, query_grads, basis_in, basis_out, eigvals.T)
    return (scores.T * (1.0 / math.sqrt(D * H)), energies.reshape(2) / (D * H))


def solution(mesh):
    return jax.shard_map(
        on_device,
        mesh=mesh,
        in_specs=(
            P("dp", "mp"),
            P("dp", "mp"),
            P("dp", "mp"),
            P("dp", "mp"),
            P("mp", None),
            P("mp", None),
            P(None, "mp"),
        ),
        out_specs=(P(None, "dp"), P("dp")),
        check_vma=False,
    )
```
